32 devices in a mesh: xy: 2 (over core), gz: 16 (over z, y, x).
Axes of the slice: x: 2, y: 2, z: 4, core: 2. Of those that a mesh axis runs over, the one named last changes fastest.
Arguments:
- volume: bfloat16 [4, 128, 128, 128], P('xy', None, 'gz'), may hold values from -6 to 6
- conv_first: bfloat16 [3, 3, 128, 128], replicated, may hold values from -0.1875 to 0.1875
- conv_second: bfloat16 [3, 3, 128, 128], replicated, may hold values from -0.1875 to 0.1875
- w_qkv: bfloat16 [128, 384], replicated
- w_out: bfloat16 [128, 128], replicated, may hold values from -0.5 to 0.5
Outputs:
- refined: bfloat16 [4, 128, 128, 128], P('xy', None, 'gz')
The draws below stay inside these ranges and needn't reach their ends.
All inputs are finite; a program needn't handle non-finite values.
Results may differ from the reference program's by a relative error of at most 0.0085.
Values may be sent and summed in bfloat16 or wider, within the bound.
A program may use at most 64 MiB of HBM per device.

```python
import math
import jax
import jax.numpy as jnp
from jax import lax

CH = 128
HEADS = 4
WIDE = 128
ROWS = 4
SECTIONS = 128


def draw_w_qkv(key, part):
    base = jax.random.normal(key, (CH, 3 * CH), jnp.float32) / math.sqrt(CH)
    return base.astype(jnp.bfloat16)


def block_scale(key, dims, split, low, top_value):
    loudness = 1.0
    for axis_at, blocks in split:
        heights = jax.random.uniform(jax.random.fold_in(jax.random.fold_in(key, 6), axis_at), (blocks,), jnp.float32, low / len(split), top_value / len(split))
        loudness = loudness * jnp.repeat(jnp.exp(heights), dims[axis_at] // blocks).reshape((-1,) + (1,) * (len(dims) - 1 - axis_at))
    return loudness


def bell_draw(stream_key, dims, deviation, limit, pieces=(), kind=jnp.bfloat16):
    loudness = block_scale(stream_key, dims, pieces, -0.22, 0.18) if pieces else 1.0
    entries = jax.random.normal(stream_key, dims, jnp.float32) * deviation * loudness
    return jnp.minimum(jnp.maximum(entries, -limit), limit).astype(kind)


def setup_inputs(seed: int = 0) -> dict:
    streams_of = jax.random.split(jax.random.key(seed), 6)
    return {
        "volume": bell_draw(streams_of[0], (ROWS, WIDE, SECTIONS, CH), 1.0, 6.0, ((0, 2), (2, 16))),
        "conv_first": bell_draw(streams_of[1], (3, 3, CH, CH), (9 * CH) ** -0.5, 0.1875),
        "conv_second": bell_draw(streams_of[2], (3, 3, CH, CH), (9 * CH) ** -0.5, 0.1875),
        "w_qkv": draw_w_qkv(jax.random.fold_in(streams_of[5], 71), 0),
        "w_out": bell_draw(streams_of[4], (CH, CH), CH ** -0.5, 0.5),
    }


def conv_all(field, weight, finish):
    count = field.shape[0]
    cols = field.shape[1]
    padded = jnp.pad(field, ((1, 1), (1, 1), (0, 0), (0, 0)))

    def one_row(index):
        rows = lax.dynamic_slice_in_dim(padded, index, 3, 0)
        total = jnp.zeros(field.shape[1:], jnp.float32)
        for shift_r in range(3):
            for shift_c in range(3):
                total = total + jnp.dot(rows[shift_r, shift_c:shift_c + cols], weight[shift_r, shift_c], preferred_element_type=jnp.float32)
        return finish(total, index)
    return lax.map(one_row, jnp.arange(count, dtype=jnp.int32))

def attend_row(row, w_qkv, w_out):
    cols, depth, width = row.shape
    values = row.astype(jnp.float32)
    normed = values / jnp.sqrt(lax.optimization_barrier(jnp.mean(values * values, axis=-1, keepdims=True)) + 1e-06)
    qkv = jnp.dot(normed.reshape(cols * depth, width), w_qkv.astype(jnp.float32), preferred_element_type=jnp.float32).astype(jnp.bfloat16)
    qkv = qkv.reshape(cols, depth, 3, HEADS, width // HEADS).astype(jnp.float32)
    scores = jnp.einsum('cqhd,ckhd->chqk', qkv[:, :, 0], qkv[:, :, 1]) / jnp.sqrt(jnp.float32(width // HEADS))
    probs = jax.nn.softmax(scores, axis=-1).astype(jnp.bfloat16)
    context = jnp.einsum('chqk,ckhd->cqhd', probs.astype(jnp.float32), qkv[:, :, 2]).astype(jnp.bfloat16)
    attended = jnp.dot(context.reshape(cols * depth, width), w_out, preferred_element_type=jnp.float32).astype(jnp.bfloat16)
    return attended.reshape(cols, depth, width)

def reference(volume, conv_first, conv_second, w_qkv, w_out):
    hidden = conv_all(volume, conv_first, lambda total, index: jax.nn.silu(total).astype(jnp.bfloat16))

    def add_back(total, index):
        base = lax.dynamic_index_in_dim(volume, index, 0, keepdims=False)
        return (base.astype(jnp.float32) + total).astype(jnp.bfloat16)
    mixed = conv_all(hidden, conv_second, add_back)

    def finish_row(row):
        attended = attend_row(row, w_qkv, w_out)
        return (row.astype(jnp.float32) + attended.astype(jnp.float32)).astype(jnp.bfloat16)
    return lax.map(finish_row, mixed)
```

```python
import functools
import math

import jax
import jax.numpy as jnp
from jax import lax
from jax.experimental import pallas as pl
from jax.experimental.pallas import tpu as pltpu
from jax.sharding import PartitionSpec as P

HEADS = 4
CHUNKS = 4
MESH = pl.DeviceIdType.MESH
F32 = jnp.float32
BF16 = jnp.bfloat16


def fill_pairs(wide_ref, weight_ref, ch):
    for out_row in range(2):
        for shift_c in range(3):
            col = (out_row * 3 + shift_c) * ch
            for in_row in range(4):
                shift_r = in_row - out_row
                rows = pl.ds(in_row * ch, ch)
                if 0 <= shift_r < 3:
                    wide_ref[rows, pl.ds(col, ch)] = weight_ref[shift_r, shift_c]
                else:
                    wide_ref[rows, pl.ds(col, ch)] = jnp.zeros((ch, ch), BF16)


def conv_pair(src_ref, row, start, size, wide_ref, ch, sz):
    span = pl.ds(start - 2 * sz, size + 4 * sz)
    rows = jnp.concatenate([src_ref[row + i, span, :] for i in range(4)], axis=-1)
    parts = jnp.dot(rows, wide_ref[...], preferred_element_type=F32)
    outs = []
    for out_row in range(2):
        total = None
        for shift_c in range(3):
            col = (out_row * 3 + shift_c) * ch
            at = 2 * sz + (shift_c - 1) * sz
            part = parts[at : at + size, col : col + ch]
            total = part if total is None else total + part
        outs.append(total)
    return outs


def kernel(
    n, np_, vol, w1, w2, wqkv, wout, out,
    vpad, hpad, mixed, wide1, wide2, recv, att, ret,
    load_sem, halo_send, halo_recv, fwd_send, fwd_recv, own_sem, bwd_send, bwd_recv,
):
    count, flat, ch = mixed.shape
    cells = flat // CHUNKS
    unit = cells // n
    sz = unit // 2
    pad = 2 * sz
    me = lax.axis_index("gz")
    p = lax.axis_index("xy")

    load = pltpu.make_async_copy(vol, vpad.at[pl.ds(2, count), pl.ds(pad, flat)], load_sem)
    load.start()

    barrier = pltpu.get_barrier_semaphore()
    for d in range(1, n):
        pl.semaphore_signal(barrier, inc=1, device_id={"gz": lax.rem(me + d, n)}, device_id_type=MESH)

    @pl.when(p > 0)
    def _():
        pl.semaphore_signal(barrier, inc=1, device_id={"xy": p - 1}, device_id_type=MESH)

    @pl.when(p < np_ - 1)
    def _():
        pl.semaphore_signal(barrier, inc=1, device_id={"xy": p + 1}, device_id_type=MESH)

    edge = jnp.zeros((pad, ch), BF16)
    for row in range(count + 4):
        vpad[row, pl.ds(0, pad), :] = edge
        vpad[row, pl.ds(pad + flat, pad), :] = edge
    for row in range(count + 2):
        hpad[row, pl.ds(0, pad), :] = edge
        hpad[row, pl.ds(pad + flat, pad), :] = edge

    @pl.when(p == 0)
    def _():
        vpad[pl.ds(0, 2), pl.ds(pad, flat), :] = jnp.zeros((2, flat, ch), BF16)

    @pl.when(p == np_ - 1)
    def _():
        vpad[pl.ds(count + 2, 2), pl.ds(pad, flat), :] = jnp.zeros((2, flat, ch), BF16)

    extra = jnp.where(p > 0, 1, 0) + jnp.where(p < np_ - 1, 1, 0)
    pl.semaphore_wait(barrier, n - 1 + extra)

    up = pltpu.make_async_remote_copy(
        src_ref=vol.at[pl.ds(0, 2)], dst_ref=vpad.at[pl.ds(count + 2, 2), pl.ds(pad, flat)],
        send_sem=halo_send.at[0], recv_sem=halo_recv.at[0],
        device_id={"xy": p - 1}, device_id_type=MESH,
    )
    down = pltpu.make_async_remote_copy(
        src_ref=vol.at[pl.ds(count - 2, 2)], dst_ref=vpad.at[pl.ds(0, 2), pl.ds(pad, flat)],
        send_sem=halo_send.at[1], recv_sem=halo_recv.at[1],
        device_id={"xy": p + 1}, device_id_type=MESH,
    )

    @pl.when(p > 0)
    def _():
        up.start()

    @pl.when(p < np_ - 1)
    def _():
        down.start()

    fill_pairs(wide1, w1, ch)
    fill_pairs(wide2, w2, ch)
    load.wait()

    @pl.when(p > 0)
    def _():
        up.wait_send()
        down.wait_recv()

    @pl.when(p < np_ - 1)
    def _():
        down.wait_send()
        up.wait_recv()

    done = 0
    for k in range(CHUNKS):
        upto = min((k + 1) * cells + pad, flat)
        size = upto - done
        for pair in range((count + 2) // 2):
            pieces = conv_pair(vpad, 2 * pair, pad + done, size, wide1, ch, sz)
            for i, first in enumerate(pieces):
                row = 2 * pair + i
                half = 0.5 * first
                value = half + half * jnp.tanh(half)
                if row == 0:
                    value = jnp.where(p > 0, value, 0.0)
                if row == count + 1:
                    value = jnp.where(p < np_ - 1, value, 0.0)
                hpad[row, pl.ds(pad + done, size), :] = value.astype(BF16)
        done = upto
        for pair in range(count // 2):
            pieces = conv_pair(hpad, 2 * pair, pad + k * cells, cells, wide2, ch, sz)
            for i, second in enumerate(pieces):
                row = 2 * pair + i
                base = vpad[row + 2, pl.ds(pad + k * cells, cells), :].astype(F32)
                mixed[row, pl.ds(k * cells, cells), :] = (base + second).astype(BF16)
        for d in range(1, n):
            to = lax.rem(me + d, n)
            start = pl.multiple_of(k * cells + to * unit, unit)
            pltpu.make_async_remote_copy(
                src_ref=mixed.at[:, pl.ds(start, unit)], dst_ref=recv.at[k, me],
                send_sem=fwd_send.at[k], recv_sem=fwd_recv.at[k],
                device_id={"gz": to}, device_id_type=MESH,
            ).start()
        start = pl.multiple_of(k * cells + me * unit, unit)
        pltpu.make_async_copy(mixed.at[:, pl.ds(start, unit)], recv.at[k, me], own_sem.at[k]).start()

    width = ch // HEADS
    lane = lax.broadcasted_iota(jnp.int32, (n * sz, ch), 1) // width
    masks = [jnp.where(lane == h, 1.0, 0.0).astype(BF16) for h in range(HEADS)]
    ones = jnp.concatenate(masks, axis=0)
    factor = math.log2(math.e) / math.sqrt(width)
    depth = n * sz
    for k in range(CHUNKS):
        others = recv.at[k, pl.ds(0, n - 1)]
        pltpu.make_async_copy(others, others, fwd_recv.at[k]).wait()
        pltpu.make_async_copy(recv.at[k, 0], recv.at[k, 0], own_sem.at[k]).wait()
        for r in range(count):
            block = recv[k, :, r].astype(F32).reshape(n, 2, sz, ch)
            x = jnp.concatenate([block[:, j].reshape(depth, ch) for j in range(2)], axis=0)
            inv = lax.rsqrt(jnp.mean(x * x, axis=-1, keepdims=True) + 1e-6)
            qkv = (jnp.dot(x.astype(BF16), wqkv[...], preferred_element_type=F32) * inv).astype(BF16)
            contexts = []
            for j in range(2):
                q = qkv[j * depth : (j + 1) * depth, :ch]
                key = qkv[j * depth : (j + 1) * depth, ch : 2 * ch]
                v = qkv[j * depth : (j + 1) * depth, 2 * ch :]
                keys = jnp.concatenate([key * m for m in masks], axis=0)
                scores = lax.dot_general(q, keys, (((1,), (1,)), ((), ())), preferred_element_type=F32)
                probs = []
                for h in range(HEADS):
                    s = scores[:, h * depth : (h + 1) * depth]
                    top = jnp.max(s, axis=-1, keepdims=True)
                    probs.append(jnp.exp2((s - top) * factor).astype(BF16))
                values = jnp.concatenate([jnp.concatenate([v * m for m in masks], axis=0), ones], axis=1)
                sums = jnp.dot(jnp.concatenate(probs, axis=1), values, preferred_element_type=F32)
                contexts.append((sums[:, :ch] / sums[:, ch:]).astype(BF16))
            a = jnp.dot(jnp.concatenate(contexts, axis=0), wout[...], preferred_element_type=F32)
            a = jnp.stack([a[:depth].reshape(n, sz, ch), a[depth:].reshape(n, sz, ch)], axis=1)
            att[k, :, r] = a.reshape(n, 2 * sz, ch).astype(BF16)
        spot = pl.multiple_of(k * cells + me * unit, unit)
        for d in range(1, n):
            to = lax.rem(me + d, n)
            pltpu.make_async_remote_copy(
                src_ref=att.at[k, to], dst_ref=ret.at[:, pl.ds(spot, unit)],
                send_sem=bwd_send.at[k], recv_sem=bwd_recv.at[k],
                device_id={"gz": to}, device_id_type=MESH,
            ).start()
        pltpu.make_async_copy(att.at[k, me], ret.at[:, pl.ds(spot, unit)], own_sem.at[k]).start()

    for k in range(CHUNKS):
        others = recv.at[k, pl.ds(0, n - 1)]
        pltpu.make_async_copy(others, others, bwd_recv.at[k]).wait()
        pltpu.make_async_copy(recv.at[k, 0], recv.at[k, 0], own_sem.at[k]).wait()
        span = pl.ds(k * cells, cells)
        for r in range(count):
            out[r, span, :] = (mixed[r, span, :].astype(F32) + ret[r, span, :].astype(F32)).astype(BF16)
    for k in range(CHUNKS):
        others = recv.at[k, pl.ds(0, n - 1)]
        pltpu.make_async_copy(others, others, fwd_send.at[k]).wait()
        pltpu.make_async_copy(others, others, bwd_send.at[k]).wait()


def on_device(volume, conv_first, conv_second, w_qkv, w_out):
    count, wide, sz, ch = volume.shape
    n, np_ = lax.axis_size("gz"), lax.axis_size("xy")
    flat = wide * sz
    unit = flat // CHUNKS // n
    vmem = pl.BlockSpec(memory_space=pltpu.VMEM)
    pad = 2 * sz
    out = pl.pallas_call(
        functools.partial(kernel, n, np_),
        out_shape=jax.ShapeDtypeStruct((count, flat, ch), BF16),
        in_specs=[pl.BlockSpec(memory_space=pl.ANY)] + [vmem] * 4,
        out_specs=vmem,
        scratch_shapes=[
            pltpu.VMEM((count + 4, flat + 2 * pad, ch), BF16),
            pltpu.VMEM((count + 2, flat + 2 * pad, ch), BF16),
            pltpu.VMEM((count, flat, ch), BF16),
            pltpu.VMEM((4 * ch, 6 * ch), BF16),
            pltpu.VMEM((4 * ch, 6 * ch), BF16),
            pltpu.VMEM((CHUNKS, n, count, unit, ch), BF16),
            pltpu.VMEM((CHUNKS, n, count, unit, ch), BF16),
            pltpu.VMEM((count, flat, ch), BF16),
            pltpu.SemaphoreType.DMA(()),
            pltpu.SemaphoreType.DMA((2,)),
            pltpu.SemaphoreType.DMA((2,)),
            pltpu.SemaphoreType.DMA((CHUNKS,)),
            pltpu.SemaphoreType.DMA((CHUNKS,)),
            pltpu.SemaphoreType.DMA((CHUNKS,)),
            pltpu.SemaphoreType.DMA((CHUNKS,)),
            pltpu.SemaphoreType.DMA((CHUNKS,)),
        ],
        compiler_params=pltpu.CompilerParams(
            collective_id=0, has_side_effects=True, vmem_limit_bytes=48 * 1024 * 1024
        ),
        cost_estimate=pl.CostEstimate(
            flops=2 * count * flat * ch * ch * 24, bytes_accessed=4 * count * flat * ch, transcendentals=0
        ),
    )(volume.reshape(count, flat, ch), conv_first, conv_second, w_qkv, w_out)
    return out.reshape(volume.shape)


def solution(mesh):
    placed = (P("xy", None, "gz", None), P(), P(), P(), P())
    return jax.shard_map(
        on_device, mesh=mesh, in_specs=placed, out_specs=P("xy", None, "gz", None), check_vma=False
    )
```

```python
import functools
import math

import jax
import jax.numpy as jnp
from jax import lax
from jax.experimental import pallas as pl
from jax.experimental.pallas import tpu as pltpu
from jax.sharding import PartitionSpec as P

HEADS = 4
CHUNKS = 4
MESH = pl.DeviceIdType.MESH
F32 = jnp.float32
BF16 = jnp.bfloat16


def fill_pairs(wide_ref, weight_ref, ch):
    for out_row in range(2):
        for shift_c in range(3):
            col = (out_row * 3 + shift_c) * ch
            for in_row in range(4):
                shift_r = in_row - out_row
                rows = pl.ds(in_row * ch, ch)
                if 0 <= shift_r < 3:
                    wide_ref[rows, pl.ds(col, ch)] = weight_ref[shift_r, shift_c]
                else:
                    wide_ref[rows, pl.ds(col, ch)] = jnp.zeros((ch, ch), BF16)


def conv_pair(src_ref, row, start, size, wide_ref, ch, sz):
    span = pl.ds(start - 2 * sz, size + 4 * sz)
    rows = jnp.concatenate([src_ref[row + i, span, :] for i in range(4)], axis=-1)
    parts = jnp.dot(rows, wide_ref[...], preferred_element_type=F32)
    outs = []
    for out_row in range(2):
        total = None
        for shift_c in range(3):
            col = (out_row * 3 + shift_c) * ch
            at = 2 * sz + (shift_c - 1) * sz
            part = parts[at : at + size, col : col + ch]
            total = part if total is None else total + part
        outs.append(total)
    return outs


def kernel(
    n, np_, vol, w1_in, w2_in, wqkv_in, wout_in, out,
    w1, w2, wqkv, wout,
    vpad, hpad, mixed, wide1, wide2, recv, att, ret,
    load_sem, weight_sem, halo_send, halo_recv, fwd_send, fwd_recv, own_sem, bwd_send, bwd_recv,
):
    count, flat, ch = mixed.shape
    cells = flat // CHUNKS
    unit = cells // n
    sz = unit // 2
    pad = 2 * sz
    me = lax.axis_index("gz")
    p = lax.axis_index("xy")

    load = pltpu.make_async_copy(vol, vpad.at[pl.ds(2, count), pl.ds(pad, flat)], load_sem)
    load.start()
    weights = [
        pltpu.make_async_copy(src, dst, weight_sem.at[i])
        for i, (src, dst) in enumerate(((w1_in, w1), (w2_in, w2), (wqkv_in, wqkv), (wout_in, wout)))
    ]
    for copy in weights:
        copy.start()

    barrier = pltpu.get_barrier_semaphore()
    for d in range(1, n):
        pl.semaphore_signal(barrier, inc=1, device_id={"gz": lax.rem(me + d, n)}, device_id_type=MESH)

    @pl.when(p > 0)
    def _():
        pl.semaphore_signal(barrier, inc=1, device_id={"xy": p - 1}, device_id_type=MESH)

    @pl.when(p < np_ - 1)
    def _():
        pl.semaphore_signal(barrier, inc=1, device_id={"xy": p + 1}, device_id_type=MESH)

    edge = jnp.zeros((pad, ch), BF16)
    for row in range(count + 4):
        vpad[row, pl.ds(0, pad), :] = edge
        vpad[row, pl.ds(pad + flat, pad), :] = edge
    for row in range(count + 2):
        hpad[row, pl.ds(0, pad), :] = edge
        hpad[row, pl.ds(pad + flat, pad), :] = edge

    @pl.when(p == 0)
    def _():
        vpad[pl.ds(0, 2), pl.ds(pad, flat), :] = jnp.zeros((2, flat, ch), BF16)

    @pl.when(p == np_ - 1)
    def _():
        vpad[pl.ds(count + 2, 2), pl.ds(pad, flat), :] = jnp.zeros((2, flat, ch), BF16)

    extra = jnp.where(p > 0, 1, 0) + jnp.where(p < np_ - 1, 1, 0)
    pl.semaphore_wait(barrier, n - 1 + extra)

    up = pltpu.make_async_remote_copy(
        src_ref=vol.at[pl.ds(0, 2)], dst_ref=vpad.at[pl.ds(count + 2, 2), pl.ds(pad, flat)],
        send_sem=halo_send.at[0], recv_sem=halo_recv.at[0],
        device_id={"xy": p - 1}, device_id_type=MESH,
    )
    down = pltpu.make_async_remote_copy(
        src_ref=vol.at[pl.ds(count - 2, 2)], dst_ref=vpad.at[pl.ds(0, 2), pl.ds(pad, flat)],
        send_sem=halo_send.at[1], recv_sem=halo_recv.at[1],
        device_id={"xy": p + 1}, device_id_type=MESH,
    )

    @pl.when(p > 0)
    def _():
        up.start()

    @pl.when(p < np_ - 1)
    def _():
        down.start()

    for copy in weights:
        copy.wait()
    fill_pairs(wide1, w1, ch)
    fill_pairs(wide2, w2, ch)
    load.wait()

    @pl.when(p > 0)
    def _():
        up.wait_send()
        down.wait_recv()

    @pl.when(p < np_ - 1)
    def _():
        down.wait_send()
        up.wait_recv()

    done = 0
    for k in range(CHUNKS):
        upto = min((k + 1) * cells + pad, flat)
        size = upto - done
        for pair in range((count + 2) // 2):
            pieces = conv_pair(vpad, 2 * pair, pad + done, size, wide1, ch, sz)
            for i, first in enumerate(pieces):
                row = 2 * pair + i
                half = 0.5 * first
                value = half + half * jnp.tanh(half)
                if row == 0:
                    value = jnp.where(p > 0, value, 0.0)
                if row == count + 1:
                    value = jnp.where(p < np_ - 1, value, 0.0)
                hpad[row, pl.ds(pad + done, size), :] = value.astype(BF16)
        done = upto
        for pair in range(count // 2):
            pieces = conv_pair(hpad, 2 * pair, pad + k * cells, cells, wide2, ch, sz)
            for i, second in enumerate(pieces):
                row = 2 * pair + i
                base = vpad[row + 2, pl.ds(pad + k * cells, cells), :].astype(F32)
                mixed[row, pl.ds(k * cells, cells), :] = (base + second).astype(BF16)
        for d in range(1, n):
            to = lax.rem(me + d, n)
            start = pl.multiple_of(k * cells + to * unit, unit)
            pltpu.make_async_remote_copy(
                src_ref=mixed.at[:, pl.ds(start, unit)], dst_ref=recv.at[k, me],
                send_sem=fwd_send.at[k], recv_sem=fwd_recv.at[k],
                device_id={"gz": to}, device_id_type=MESH,
            ).start()
        start = pl.multiple_of(k * cells + me * unit, unit)
        pltpu.make_async_copy(mixed.at[:, pl.ds(start, unit)], recv.at[k, me], own_sem.at[k]).start()

    width = ch // HEADS
    lane = lax.broadcasted_iota(jnp.int32, (n * sz, ch), 1) // width
    masks = [jnp.where(lane == h, 1.0, 0.0).astype(BF16) for h in range(HEADS)]
    ones = jnp.concatenate(masks, axis=0)
    factor = math.log2(math.e) / math.sqrt(width)
    depth = n * sz
    for k in range(CHUNKS):
        others = recv.at[k, pl.ds(0, n - 1)]
        pltpu.make_async_copy(others, others, fwd_recv.at[k]).wait()
        pltpu.make_async_copy(recv.at[k, 0], recv.at[k, 0], own_sem.at[k]).wait()
        for r in range(count):
            block = recv[k, :, r].astype(F32).reshape(n, 2, sz, ch)
            x = jnp.concatenate([block[:, j].reshape(depth, ch) for j in range(2)], axis=0)
            inv = lax.rsqrt(jnp.mean(x * x, axis=-1, keepdims=True) + 1e-6)
            qkv = (jnp.dot(x.astype(BF16), wqkv[...], preferred_element_type=F32) * inv).astype(BF16)
            contexts = []
            for j in range(2):
                q = qkv[j * depth : (j + 1) * depth, :ch]
                key = qkv[j * depth : (j + 1) * depth, ch : 2 * ch]
                v = qkv[j * depth : (j + 1) * depth, 2 * ch :]
                keys = jnp.concatenate([key * m for m in masks], axis=0)
                scores = lax.dot_general(q, keys, (((1,), (1,)), ((), ())), preferred_element_type=F32)
                probs = []
                for h in range(HEADS):
                    s = scores[:, h * depth : (h + 1) * depth]
                    top = jnp.max(s, axis=-1, keepdims=True)
                    probs.append(jnp.exp2((s - top) * factor).astype(BF16))
                values = jnp.concatenate([jnp.concatenate([v * m for m in masks], axis=0), ones], axis=1)
                sums = jnp.dot(jnp.concatenate(probs, axis=1), values, preferred_element_type=F32)
                contexts.append((sums[:, :ch] / sums[:, ch:]).astype(BF16))
            a = jnp.dot(jnp.concatenate(contexts, axis=0), wout[...], preferred_element_type=F32)
            a = jnp.stack([a[:depth].reshape(n, sz, ch), a[depth:].reshape(n, sz, ch)], axis=1)
            att[k, :, r] = a.reshape(n, 2 * sz, ch).astype(BF16)
        spot = pl.multiple_of(k * cells + me * unit, unit)
        for d in range(1, n):
            to = lax.rem(me + d, n)
            pltpu.make_async_remote_copy(
                src_ref=att.at[k, to], dst_ref=ret.at[:, pl.ds(spot, unit)],
                send_sem=bwd_send.at[k], recv_sem=bwd_recv.at[k],
                device_id={"gz": to}, device_id_type=MESH,
            ).start()
        pltpu.make_async_copy(att.at[k, me], ret.at[:, pl.ds(spot, unit)], own_sem.at[k]).start()

    for k in range(CHUNKS):
        others = recv.at[k, pl.ds(0, n - 1)]
        pltpu.make_async_copy(others, others, bwd_recv.at[k]).wait()
        pltpu.make_async_copy(recv.at[k, 0], recv.at[k, 0], own_sem.at[k]).wait()
        span = pl.ds(k * cells, cells)
        for r in range(count):
            out[r, span, :] = (mixed[r, span, :].astype(F32) + ret[r, span, :].astype(F32)).astype(BF16)
    for k in range(CHUNKS):
        others = recv.at[k, pl.ds(0, n - 1)]
        pltpu.make_async_copy(others, others, fwd_send.at[k]).wait()
        pltpu.make_async_copy(others, others, bwd_send.at[k]).wait()


def on_device(volume, conv_first, conv_second, w_qkv, w_out):
    count, wide, sz, ch = volume.shape
    n, np_ = lax.axis_size("gz"), lax.axis_size("xy")
    flat = wide * sz
    unit = flat // CHUNKS // n
    vmem = pl.BlockSpec(memory_space=pltpu.VMEM)
    pad = 2 * sz
    out = pl.pallas_call(
        functools.partial(kernel, n, np_),
        out_shape=jax.ShapeDtypeStruct((count, flat, ch), BF16),
        in_specs=[pl.BlockSpec(memory_space=pl.ANY)] * 5,
        out_specs=vmem,
        scratch_shapes=[
            pltpu.VMEM(conv_first.shape, BF16),
            pltpu.VMEM(conv_second.shape, BF16),
            pltpu.VMEM(w_qkv.shape, BF16),
            pltpu.VMEM(w_out.shape, BF16),
            pltpu.VMEM((count + 4, flat + 2 * pad, ch), BF16),
            pltpu.VMEM((count + 2, flat + 2 * pad, ch), BF16),
            pltpu.VMEM((count, flat, ch), BF16),
            pltpu.VMEM((4 * ch, 6 * ch), BF16),
            pltpu.VMEM((4 * ch, 6 * ch), BF16),
            pltpu.VMEM((CHUNKS, n, count, unit, ch), BF16),
            pltpu.VMEM((CHUNKS, n, count, unit, ch), BF16),
            pltpu.VMEM((count, flat, ch), BF16),
            pltpu.SemaphoreType.DMA(()),
            pltpu.SemaphoreType.DMA((4,)),
            pltpu.SemaphoreType.DMA((2,)),
            pltpu.SemaphoreType.DMA((2,)),
            pltpu.SemaphoreType.DMA((CHUNKS,)),
            pltpu.SemaphoreType.DMA((CHUNKS,)),
            pltpu.SemaphoreType.DMA((CHUNKS,)),
            pltpu.SemaphoreType.DMA((CHUNKS,)),
            pltpu.SemaphoreType.DMA((CHUNKS,)),
        ],
        compiler_params=pltpu.CompilerParams(
            collective_id=0, has_side_effects=True, vmem_limit_bytes=60 * 1024 * 1024
        ),
        cost_estimate=pl.CostEstimate(
            flops=2 * count * flat * ch * ch * 24, bytes_accessed=4 * count * flat * ch, transcendentals=0
        ),
    )(volume.reshape(count, flat, ch), conv_first, conv_second, w_qkv, w_out)
    return out.reshape(volume.shape)


def solution(mesh):
    placed = (P("xy", None, "gz", None), P(), P(), P(), P())
    return jax.shard_map(
        on_device, mesh=mesh, in_specs=placed, out_specs=P("xy", None, "gz", None), check_vma=False
    )
```

```python
import functools
import math

import jax
import jax.numpy as jnp
from jax import lax
from jax.experimental import pallas as pl
from jax.experimental.pallas import tpu as pltpu
from jax.sharding import PartitionSpec as P

HEADS = 4
CHUNKS = 4
MESH = pl.DeviceIdType.MESH
F32 = jnp.float32
BF16 = jnp.bfloat16


def fill_pairs(wide_ref, weight_ref, ch):
    for out_row in range(2):
        for shift_c in range(3):
            col = (out_row * 3 + shift_c) * ch
            for in_row in range(4):
                shift_r = in_row - out_row
                rows = pl.ds(in_row * ch, ch)
                if 0 <= shift_r < 3:
                    wide_ref[rows, pl.ds(col, ch)] = weight_ref[shift_r, shift_c]
                else:
                    wide_ref[rows, pl.ds(col, ch)] = jnp.zeros((ch, ch), BF16)


def conv_pair(src_ref, row, start, size, wide_ref, ch, sz):
    span = pl.ds(start - 2 * sz, size + 4 * sz)
    rows = jnp.concatenate([src_ref[row + i, span, :] for i in range(4)], axis=-1)
    parts = jnp.dot(rows, wide_ref[...], preferred_element_type=F32)
    outs = []
    for out_row in range(2):
        total = None
        for shift_c in range(3):
            col = (out_row * 3 + shift_c) * ch
            at = 2 * sz + (shift_c - 1) * sz
            part = parts[at : at + size, col : col + ch]
            total = part if total is None else total + part
        outs.append(total)
    return outs


def kernel(
    n, np_, vol, w1_in, w2_in, wqkv_in, wout_in, out,
    w1, w2, wqkv, wout,
    vpad, hpad, mixed, wide1, wide2, recv, att, ret,
    load_sem, weight_sem, halo_send, halo_recv, fwd_send, fwd_recv, own_sem, bwd_send, bwd_recv,
):
    count, flat, ch = mixed.shape
    cells = flat // CHUNKS
    unit = cells // n
    sz = unit // 2
    pad = 2 * sz
    me = lax.axis_index("gz")
    p = lax.axis_index("xy")

    load = pltpu.make_async_copy(vol, vpad.at[pl.ds(2, count), pl.ds(pad, flat)], load_sem)
    load.start()
    weights = [
        pltpu.make_async_copy(src, dst, weight_sem.at[i])
        for i, (src, dst) in enumerate(((w1_in, w1), (w2_in, w2), (wqkv_in, wqkv), (wout_in, wout)))
    ]
    for copy in weights:
        copy.start()

    barrier = pltpu.get_barrier_semaphore()
    for d in range(1, n):
        pl.semaphore_signal(barrier, inc=1, device_id={"gz": lax.rem(me + d, n)}, device_id_type=MESH)

    @pl.when(p > 0)
    def _():
        pl.semaphore_signal(barrier, inc=1, device_id={"xy": p - 1}, device_id_type=MESH)

    @pl.when(p < np_ - 1)
    def _():
        pl.semaphore_signal(barrier, inc=1, device_id={"xy": p + 1}, device_id_type=MESH)

    edge = jnp.zeros((pad, ch), BF16)
    for row in range(count + 4):
        vpad[row, pl.ds(0, pad), :] = edge
        vpad[row, pl.ds(pad + flat, pad), :] = edge
    for row in range(count + 2):
        hpad[row, pl.ds(0, pad), :] = edge
        hpad[row, pl.ds(pad + flat, pad), :] = edge

    @pl.when(p == 0)
    def _():
        vpad[pl.ds(0, 2), pl.ds(pad, flat), :] = jnp.zeros((2, flat, ch), BF16)

    @pl.when(p == np_ - 1)
    def _():
        vpad[pl.ds(count + 2, 2), pl.ds(pad, flat), :] = jnp.zeros((2, flat, ch), BF16)

    extra = jnp.where(p > 0, 1, 0) + jnp.where(p < np_ - 1, 1, 0)
    pl.semaphore_wait(barrier, n - 1 + extra)

    marks = [0] + [min((k + 1) * cells + 2 * pad, flat) for k in range(CHUNKS)]
    ups, downs = [], []
    for k in range(CHUNKS):
        span, held = pl.ds(marks[k], marks[k + 1] - marks[k]), pl.ds(pad + marks[k], marks[k + 1] - marks[k])
        ups.append(pltpu.make_async_remote_copy(
            src_ref=vol.at[pl.ds(0, 2), span], dst_ref=vpad.at[pl.ds(count + 2, 2), held],
            send_sem=halo_send.at[0, k], recv_sem=halo_recv.at[0, k],
            device_id={"xy": p - 1}, device_id_type=MESH,
        ))
        downs.append(pltpu.make_async_remote_copy(
            src_ref=vol.at[pl.ds(count - 2, 2), span], dst_ref=vpad.at[pl.ds(0, 2), held],
            send_sem=halo_send.at[1, k], recv_sem=halo_recv.at[1, k],
            device_id={"xy": p + 1}, device_id_type=MESH,
        ))

    @pl.when(p > 0)
    def _():
        for up in ups:
            up.start()

    @pl.when(p < np_ - 1)
    def _():
        for down in downs:
            down.start()

    for copy in weights:
        copy.wait()
    fill_pairs(wide1, w1, ch)
    fill_pairs(wide2, w2, ch)
    load.wait()

    done = 0
    for k in range(CHUNKS):
        @pl.when(p > 0)
        def _():
            downs[k].wait_recv()

        @pl.when(p < np_ - 1)
        def _():
            ups[k].wait_recv()

        upto = min((k + 1) * cells + pad, flat)
        size = upto - done
        for pair in range((count + 2) // 2):
            pieces = conv_pair(vpad, 2 * pair, pad + done, size, wide1, ch, sz)
            for i, first in enumerate(pieces):
                row = 2 * pair + i
                half = 0.5 * first
                value = half + half * jnp.tanh(half)
                if row == 0:
                    value = jnp.where(p > 0, value, 0.0)
                if row == count + 1:
                    value = jnp.where(p < np_ - 1, value, 0.0)
                hpad[row, pl.ds(pad + done, size), :] = value.astype(BF16)
        done = upto
        for pair in range(count // 2):
            pieces = conv_pair(hpad, 2 * pair, pad + k * cells, cells, wide2, ch, sz)
            for i, second in enumerate(pieces):
                row = 2 * pair + i
                base = vpad[row + 2, pl.ds(pad + k * cells, cells), :].astype(F32)
                mixed[row, pl.ds(k * cells, cells), :] = (base + second).astype(BF16)
        for d in range(1, n):
            to = lax.rem(me + d, n)
            start = pl.multiple_of(k * cells + to * unit, unit)
            pltpu.make_async_remote_copy(
                src_ref=mixed.at[:, pl.ds(start, unit)], dst_ref=recv.at[k, me],
                send_sem=fwd_send.at[k], recv_sem=fwd_recv.at[k],
                device_id={"gz": to}, device_id_type=MESH,
            ).start()
        start = pl.multiple_of(k * cells + me * unit, unit)
        pltpu.make_async_copy(mixed.at[:, pl.ds(start, unit)], recv.at[k, me], own_sem.at[k]).start()

    width = ch // HEADS
    lane = lax.broadcasted_iota(jnp.int32, (n * sz, ch), 1) // width
    masks = [jnp.where(lane == h, 1.0, 0.0).astype(BF16) for h in range(HEADS)]
    ones = jnp.concatenate(masks, axis=0)
    factor = math.log2(math.e) / math.sqrt(width)
    depth = n * sz
    for k in range(CHUNKS):
        others = recv.at[k, pl.ds(0, n - 1)]
        pltpu.make_async_copy(others, others, fwd_recv.at[k]).wait()
        pltpu.make_async_copy(recv.at[k, 0], recv.at[k, 0], own_sem.at[k]).wait()
        for r in range(count):
            block = recv[k, :, r].astype(F32).reshape(n, 2, sz, ch)
            x = jnp.concatenate([block[:, j].reshape(depth, ch) for j in range(2)], axis=0)
            inv = lax.rsqrt(jnp.mean(x * x, axis=-1, keepdims=True) + 1e-6)
            qkv = (jnp.dot(x.astype(BF16), wqkv[...], preferred_element_type=F32) * inv).astype(BF16)
            contexts = []
            for j in range(2):
                q = qkv[j * depth : (j + 1) * depth, :ch]
                key = qkv[j * depth : (j + 1) * depth, ch : 2 * ch]
                v = qkv[j * depth : (j + 1) * depth, 2 * ch :]
                keys = jnp.concatenate([key * m for m in masks], axis=0)
                scores = lax.dot_general(q, keys, (((1,), (1,)), ((), ())), preferred_element_type=F32)
                probs = []
                for h in range(HEADS):
                    s = scores[:, h * depth : (h + 1) * depth]
                    top = jnp.max(s, axis=-1, keepdims=True)
                    probs.append(jnp.exp2((s - top) * factor).astype(BF16))
                values = jnp.concatenate([jnp.concatenate([v * m for m in masks], axis=0), ones], axis=1)
                sums = jnp.dot(jnp.concatenate(probs, axis=1), values, preferred_element_type=F32)
                contexts.append((sums[:, :ch] / sums[:, ch:]).astype(BF16))
            a = jnp.dot(jnp.concatenate(contexts, axis=0), wout[...], preferred_element_type=F32)
            a = jnp.stack([a[:depth].reshape(n, sz, ch), a[depth:].reshape(n, sz, ch)], axis=1)
            att[k, :, r] = a.reshape(n, 2 * sz, ch).astype(BF16)
        spot = pl.multiple_of(k * cells + me * unit, unit)
        for d in range(1, n):
            to = lax.rem(me + d, n)
            pltpu.make_async_remote_copy(
                src_ref=att.at[k, to], dst_ref=ret.at[:, pl.ds(spot, unit)],
                send_sem=bwd_send.at[k], recv_sem=bwd_recv.at[k],
                device_id={"gz": to}, device_id_type=MESH,
            ).start()
        pltpu.make_async_copy(att.at[k, me], ret.at[:, pl.ds(spot, unit)], own_sem.at[k]).start()

    for k in range(CHUNKS):
        others = recv.at[k, pl.ds(0, n - 1)]
        pltpu.make_async_copy(others, others, bwd_recv.at[k]).wait()
        pltpu.make_async_copy(recv.at[k, 0], recv.at[k, 0], own_sem.at[k]).wait()
        span = pl.ds(k * cells, cells)
        for r in range(count):
            out[r, span, :] = (mixed[r, span, :].astype(F32) + ret[r, span, :].astype(F32)).astype(BF16)
    @pl.when(p > 0)
    def _():
        for up in ups:
            up.wait_send()

    @pl.when(p < np_ - 1)
    def _():
        for down in downs:
            down.wait_send()

    for k in range(CHUNKS):
        others = recv.at[k, pl.ds(0, n - 1)]
        pltpu.make_async_copy(others, others, fwd_send.at[k]).wait()
        pltpu.make_async_copy(others, others, bwd_send.at[k]).wait()


def on_device(volume, conv_first, conv_second, w_qkv, w_out):
    count, wide, sz, ch = volume.shape
    n, np_ = lax.axis_size("gz"), lax.axis_size("xy")
    flat = wide * sz
    unit = flat // CHUNKS // n
    vmem = pl.BlockSpec(memory_space=pltpu.VMEM)
    pad = 2 * sz
    out = pl.pallas_call(
        functools.partial(kernel, n, np_),
        out_shape=jax.ShapeDtypeStruct((count, flat, ch), BF16),
        in_specs=[pl.BlockSpec(memory_space=pl.ANY)] * 5,
        out_specs=vmem,
        scratch_shapes=[
            pltpu.VMEM(conv_first.shape, BF16),
            pltpu.VMEM(conv_second.shape, BF16),
            pltpu.VMEM(w_qkv.shape, BF16),
            pltpu.VMEM(w_out.shape, BF16),
            pltpu.VMEM((count + 4, flat + 2 * pad, ch), BF16),
            pltpu.VMEM((count + 2, flat + 2 * pad, ch), BF16),
            pltpu.VMEM((count, flat, ch), BF16),
            pltpu.VMEM((4 * ch, 6 * ch), BF16),
            pltpu.VMEM((4 * ch, 6 * ch), BF16),
            pltpu.VMEM((CHUNKS, n, count, unit, ch), BF16),
            pltpu.VMEM((CHUNKS, n, count, unit, ch), BF16),
            pltpu.VMEM((count, flat, ch), BF16),
            pltpu.SemaphoreType.DMA(()),
            pltpu.SemaphoreType.DMA((4,)),
            pltpu.SemaphoreType.DMA((2, CHUNKS)),
            pltpu.SemaphoreType.DMA((2, CHUNKS)),
            pltpu.SemaphoreType.DMA((CHUNKS,)),
            pltpu.SemaphoreType.DMA((CHUNKS,)),
            pltpu.SemaphoreType.DMA((CHUNKS,)),
            pltpu.SemaphoreType.DMA((CHUNKS,)),
            pltpu.SemaphoreType.DMA((CHUNKS,)),
        ],
        compiler_params=pltpu.CompilerParams(
            collective_id=0, has_side_effects=True, vmem_limit_bytes=60 * 1024 * 1024
        ),
        cost_estimate=pl.CostEstimate(
            flops=2 * count * flat * ch * ch * 24, bytes_accessed=4 * count * flat * ch, transcendentals=0
        ),
    )(volume.reshape(count, flat, ch), conv_first, conv_second, w_qkv, w_out)
    return out.reshape(volume.shape)


def solution(mesh):
    placed = (P("xy", None, "gz", None), P(), P(), P(), P())
    return jax.shard_map(
        on_device, mesh=mesh, in_specs=placed, out_specs=P("xy", None, "gz", None), check_vma=False
    )
```

```python
import functools
import math

import jax
import jax.numpy as jnp
from jax import lax
from jax.experimental import pallas as pl
from jax.experimental.pallas import tpu as pltpu
from jax.sharding import PartitionSpec as P

HEADS = 4
CHUNKS = 4
MESH = pl.DeviceIdType.MESH
F32 = jnp.float32
BF16 = jnp.bfloat16


def fill_pairs(wide_ref, weight_ref, ch):
    for out_row in range(2):
        for shift_c in range(3):
            col = (out_row * 3 + shift_c) * ch
            for in_row in range(4):
                shift_r = in_row - out_row
                rows = pl.ds(in_row * ch, ch)
                if 0 <= shift_r < 3:
                    wide_ref[rows, pl.ds(col, ch)] = weight_ref[shift_r, shift_c]
                else:
                    wide_ref[rows, pl.ds(col, ch)] = jnp.zeros((ch, ch), BF16)


def conv_pair(src_ref, row, start, size, wide_ref, ch, sz):
    span = pl.ds(start - 2 * sz, size + 4 * sz)
    rows = jnp.concatenate([src_ref[row + i, span, :] for i in range(4)], axis=-1)
    parts = jnp.dot(rows, wide_ref[...], preferred_element_type=F32)
    outs = []
    for out_row in range(2):
        total = None
        for shift_c in range(3):
            col = (out_row * 3 + shift_c) * ch
            at = 2 * sz + (shift_c - 1) * sz
            part = parts[at : at + size, col : col + ch]
            total = part if total is None else total + part
        outs.append(total)
    return outs


def kernel(
    n, np_, vol, w1_in, w2_in, wqkv_in, wout_in, mixed_out, ret,
    w1, w2, wqkv, wout,
    vpad, hpad, mixed, wide1, wide2, recv, att,
    load_sem, weight_sem, halo_send, halo_recv, fwd_send, fwd_recv, own_sem, bwd_send, bwd_recv, keep_sem,
):
    count, flat, ch = mixed.shape
    cells = flat // CHUNKS
    unit = cells // n
    sz = unit // 2
    pad = 2 * sz
    me = lax.axis_index("gz")
    p = lax.axis_index("xy")

    load = pltpu.make_async_copy(vol, vpad.at[pl.ds(2, count), pl.ds(pad, flat)], load_sem)
    load.start()
    weights = [
        pltpu.make_async_copy(src, dst, weight_sem.at[i])
        for i, (src, dst) in enumerate(((w1_in, w1), (w2_in, w2), (wqkv_in, wqkv), (wout_in, wout)))
    ]
    for copy in weights:
        copy.start()

    barrier = pltpu.get_barrier_semaphore()
    for d in range(1, n):
        pl.semaphore_signal(barrier, inc=1, device_id={"gz": lax.rem(me + d, n)}, device_id_type=MESH)

    @pl.when(p > 0)
    def _():
        pl.semaphore_signal(barrier, inc=1, device_id={"xy": p - 1}, device_id_type=MESH)

    @pl.when(p < np_ - 1)
    def _():
        pl.semaphore_signal(barrier, inc=1, device_id={"xy": p + 1}, device_id_type=MESH)

    edge = jnp.zeros((pad, ch), BF16)
    for row in range(count + 4):
        vpad[row, pl.ds(0, pad), :] = edge
        vpad[row, pl.ds(pad + flat, pad), :] = edge
    for row in range(count + 2):
        hpad[row, pl.ds(0, pad), :] = edge
        hpad[row, pl.ds(pad + flat, pad), :] = edge

    @pl.when(p == 0)
    def _():
        vpad[pl.ds(0, 2), pl.ds(pad, flat), :] = jnp.zeros((2, flat, ch), BF16)

    @pl.when(p == np_ - 1)
    def _():
        vpad[pl.ds(count + 2, 2), pl.ds(pad, flat), :] = jnp.zeros((2, flat, ch), BF16)

    extra = jnp.where(p > 0, 1, 0) + jnp.where(p < np_ - 1, 1, 0)
    pl.semaphore_wait(barrier, n - 1 + extra)

    marks = [0] + [min((k + 1) * cells + 2 * pad, flat) for k in range(CHUNKS)]
    ups, downs = [], []
    for k in range(CHUNKS):
        span, held = pl.ds(marks[k], marks[k + 1] - marks[k]), pl.ds(pad + marks[k], marks[k + 1] - marks[k])
        ups.append(pltpu.make_async_remote_copy(
            src_ref=vol.at[pl.ds(0, 2), span], dst_ref=vpad.at[pl.ds(count + 2, 2), held],
            send_sem=halo_send.at[0, k], recv_sem=halo_recv.at[0, k],
            device_id={"xy": p - 1}, device_id_type=MESH,
        ))
        downs.append(pltpu.make_async_remote_copy(
            src_ref=vol.at[pl.ds(count - 2, 2), span], dst_ref=vpad.at[pl.ds(0, 2), held],
            send_sem=halo_send.at[1, k], recv_sem=halo_recv.at[1, k],
            device_id={"xy": p + 1}, device_id_type=MESH,
        ))

    @pl.when(p > 0)
    def _():
        for up in ups:
            up.start()

    @pl.when(p < np_ - 1)
    def _():
        for down in downs:
            down.start()

    for copy in weights:
        copy.wait()
    fill_pairs(wide1, w1, ch)
    fill_pairs(wide2, w2, ch)
    load.wait()

    done = 0
    for k in range(CHUNKS):
        @pl.when(p > 0)
        def _():
            downs[k].wait_recv()

        @pl.when(p < np_ - 1)
        def _():
            ups[k].wait_recv()

        upto = min((k + 1) * cells + pad, flat)
        size = upto - done
        for pair in range((count + 2) // 2):
            pieces = conv_pair(vpad, 2 * pair, pad + done, size, wide1, ch, sz)
            for i, first in enumerate(pieces):
                row = 2 * pair + i
                half = 0.5 * first
                value = half + half * jnp.tanh(half)
                if row == 0:
                    value = jnp.where(p > 0, value, 0.0)
                if row == count + 1:
                    value = jnp.where(p < np_ - 1, value, 0.0)
                hpad[row, pl.ds(pad + done, size), :] = value.astype(BF16)
        done = upto
        for pair in range(count // 2):
            pieces = conv_pair(hpad, 2 * pair, pad + k * cells, cells, wide2, ch, sz)
            for i, second in enumerate(pieces):
                row = 2 * pair + i
                base = vpad[row + 2, pl.ds(pad + k * cells, cells), :].astype(F32)
                mixed[row, pl.ds(k * cells, cells), :] = (base + second).astype(BF16)
        for d in range(1, n):
            to = lax.rem(me + d, n)
            start = pl.multiple_of(k * cells + to * unit, unit)
            pltpu.make_async_remote_copy(
                src_ref=mixed.at[:, pl.ds(start, unit)], dst_ref=recv.at[k, me],
                send_sem=fwd_send.at[k], recv_sem=fwd_recv.at[k],
                device_id={"gz": to}, device_id_type=MESH,
            ).start()
        span = pl.ds(k * cells, cells)
        pltpu.make_async_copy(mixed.at[:, span], mixed_out.at[:, span], keep_sem.at[k]).start()
        start = pl.multiple_of(k * cells + me * unit, unit)
        pltpu.make_async_copy(mixed.at[:, pl.ds(start, unit)], recv.at[k, me], own_sem.at[k]).start()

    width = ch // HEADS
    lane = lax.broadcasted_iota(jnp.int32, (n * sz, ch), 1) // width
    masks = [jnp.where(lane == h, 1.0, 0.0).astype(BF16) for h in range(HEADS)]
    ones = jnp.concatenate(masks, axis=0)
    factor = math.log2(math.e) / math.sqrt(width)
    depth = n * sz
    for k in range(CHUNKS):
        others = recv.at[k, pl.ds(0, n - 1)]
        pltpu.make_async_copy(others, others, fwd_recv.at[k]).wait()
        pltpu.make_async_copy(recv.at[k, 0], recv.at[k, 0], own_sem.at[k]).wait()
        for r in range(count):
            block = recv[k, :, r].astype(F32).reshape(n, 2, sz, ch)
            x = jnp.concatenate([block[:, j].reshape(depth, ch) for j in range(2)], axis=0)
            inv = lax.rsqrt(jnp.mean(x * x, axis=-1, keepdims=True) + 1e-6)
            qkv = (jnp.dot(x.astype(BF16), wqkv[...], preferred_element_type=F32) * inv).astype(BF16)
            contexts = []
            for j in range(2):
                q = qkv[j * depth : (j + 1) * depth, :ch]
                key = qkv[j * depth : (j + 1) * depth, ch : 2 * ch]
                v = qkv[j * depth : (j + 1) * depth, 2 * ch :]
                keys = jnp.concatenate([key * m for m in masks], axis=0)
                scores = lax.dot_general(q, keys, (((1,), (1,)), ((), ())), preferred_element_type=F32)
                probs = []
                for h in range(HEADS):
                    s = scores[:, h * depth : (h + 1) * depth]
                    top = jnp.max(s, axis=-1, keepdims=True)
                    probs.append(jnp.exp2((s - top) * factor).astype(BF16))
                values = jnp.concatenate([jnp.concatenate([v * m for m in masks], axis=0), ones], axis=1)
                sums = jnp.dot(jnp.concatenate(probs, axis=1), values, preferred_element_type=F32)
                contexts.append((sums[:, :ch] / sums[:, ch:]).astype(BF16))
            a = jnp.dot(jnp.concatenate(contexts, axis=0), wout[...], preferred_element_type=F32)
            a = jnp.stack([a[:depth].reshape(n, sz, ch), a[depth:].reshape(n, sz, ch)], axis=1)
            att[k, :, r] = a.reshape(n, 2 * sz, ch).astype(BF16)
        spot = pl.multiple_of(k * cells + me * unit, unit)
        for d in range(1, n):
            to = lax.rem(me + d, n)
            pltpu.make_async_remote_copy(
                src_ref=att.at[k, to], dst_ref=ret.at[:, pl.ds(spot, unit)],
                send_sem=bwd_send.at[k], recv_sem=bwd_recv.at[k],
                device_id={"gz": to}, device_id_type=MESH,
            ).start()
        pltpu.make_async_copy(att.at[k, me], ret.at[:, pl.ds(spot, unit)], own_sem.at[k]).start()

    for k in range(CHUNKS):
        others = recv.at[k, pl.ds(0, n - 1)]
        pltpu.make_async_copy(others, others, bwd_recv.at[k]).wait()
        pltpu.make_async_copy(recv.at[k, 0], recv.at[k, 0], own_sem.at[k]).wait()
        span = pl.ds(k * cells, cells)
        pltpu.make_async_copy(mixed.at[:, span], mixed_out.at[:, span], keep_sem.at[k]).wait()
    @pl.when(p > 0)
    def _():
        for up in ups:
            up.wait_send()

    @pl.when(p < np_ - 1)
    def _():
        for down in downs:
            down.wait_send()

    for k in range(CHUNKS):
        others = recv.at[k, pl.ds(0, n - 1)]
        pltpu.make_async_copy(others, others, fwd_send.at[k]).wait()
        pltpu.make_async_copy(others, others, bwd_send.at[k]).wait()


def on_device(volume, conv_first, conv_second, w_qkv, w_out):
    count, wide, sz, ch = volume.shape
    n, np_ = lax.axis_size("gz"), lax.axis_size("xy")
    flat = wide * sz
    unit = flat // CHUNKS // n
    pad = 2 * sz
    mixed, ret = pl.pallas_call(
        functools.partial(kernel, n, np_),
        out_shape=[jax.ShapeDtypeStruct((count, flat, ch), BF16)] * 2,
        in_specs=[pl.BlockSpec(memory_space=pl.ANY)] * 5,
        out_specs=[pl.BlockSpec(memory_space=pl.ANY)] * 2,
        scratch_shapes=[
            pltpu.VMEM(conv_first.shape, BF16),
            pltpu.VMEM(conv_second.shape, BF16),
            pltpu.VMEM(w_qkv.shape, BF16),
            pltpu.VMEM(w_out.shape, BF16),
            pltpu.VMEM((count + 4, flat + 2 * pad, ch), BF16),
            pltpu.VMEM((count + 2, flat + 2 * pad, ch), BF16),
            pltpu.VMEM((count, flat, ch), BF16),
            pltpu.VMEM((4 * ch, 6 * ch), BF16),
            pltpu.VMEM((4 * ch, 6 * ch), BF16),
            pltpu.VMEM((CHUNKS, n, count, unit, ch), BF16),
            pltpu.VMEM((CHUNKS, n, count, unit, ch), BF16),
            pltpu.SemaphoreType.DMA(()),
            pltpu.SemaphoreType.DMA((4,)),
            pltpu.SemaphoreType.DMA((2, CHUNKS)),
            pltpu.SemaphoreType.DMA((2, CHUNKS)),
            pltpu.SemaphoreType.DMA((CHUNKS,)),
            pltpu.SemaphoreType.DMA((CHUNKS,)),
            pltpu.SemaphoreType.DMA((CHUNKS,)),
            pltpu.SemaphoreType.DMA((CHUNKS,)),
            pltpu.SemaphoreType.DMA((CHUNKS,)),
            pltpu.SemaphoreType.DMA((CHUNKS,)),
        ],
        compiler_params=pltpu.CompilerParams(
            collective_id=0, has_side_effects=True, vmem_limit_bytes=60 * 1024 * 1024
        ),
        cost_estimate=pl.CostEstimate(
            flops=2 * count * flat * ch * ch * 24, bytes_accessed=4 * count * flat * ch, transcendentals=0
        ),
    )(volume.reshape(count, flat, ch), conv_first, conv_second, w_qkv, w_out)
    out = (mixed.astype(F32) + ret.astype(F32)).astype(BF16)
    return out.reshape(volume.shape)


def solution(mesh):
    placed = (P("xy", None, "gz", None), P(), P(), P(), P())
    return jax.shard_map(
        on_device, mesh=mesh, in_specs=placed, out_specs=P("xy", None, "gz", None), check_vma=False
    )
```

```python
import functools
import math

import jax
import jax.numpy as jnp
from jax import lax
from jax.experimental import pallas as pl
from jax.experimental.pallas import tpu as pltpu
from jax.sharding import PartitionSpec as P

HEADS = 4
CHUNKS = 4
MESH = pl.DeviceIdType.MESH
F32 = jnp.float32
BF16 = jnp.bfloat16


def fill_pairs(wide_ref, weight_ref, ch):
    for out_row in range(2):
        for shift_c in range(3):
            col = (out_row * 3 + shift_c) * ch
            for in_row in range(4):
                shift_r = in_row - out_row
                rows = pl.ds(in_row * ch, ch)
                if 0 <= shift_r < 3:
                    wide_ref[rows, pl.ds(col, ch)] = weight_ref[shift_r, shift_c]
                else:
                    wide_ref[rows, pl.ds(col, ch)] = jnp.zeros((ch, ch), BF16)


def conv_pair(src_ref, row, start, size, wide_ref, ch, sz):
    span = pl.ds(start - 2 * sz, size + 4 * sz)
    rows = jnp.concatenate([src_ref[row + i, span, :] for i in range(4)], axis=-1)
    parts = jnp.dot(rows, wide_ref[...], preferred_element_type=F32)
    outs = []
    for out_row in range(2):
        total = None
        for shift_c in range(3):
            col = (out_row * 3 + shift_c) * ch
            at = 2 * sz + (shift_c - 1) * sz
            part = parts[at : at + size, col : col + ch]
            total = part if total is None else total + part
        outs.append(total)
    return outs


def kernel(
    n, np_, vol, w1_in, w2_in, wqkv_in, wout_in, mixed_out, ret,
    w1, w2, wqkv, wout,
    vpad, hpad, mixed, wide1, wide2, recv, att,
    load_sem, weight_sem, halo_send, halo_recv, fwd_send, fwd_recv, own_sem, bwd_send, bwd_recv, keep_sem,
):
    count, flat, ch = mixed.shape
    cells = flat // CHUNKS
    unit = cells // n
    sz = unit // 2
    pad = 2 * sz
    me = lax.axis_index("gz")
    p = lax.axis_index("xy")

    load = pltpu.make_async_copy(vol, vpad.at[pl.ds(2, count), pl.ds(pad, flat)], load_sem)
    load.start()
    weights = [
        pltpu.make_async_copy(src, dst, weight_sem.at[i])
        for i, (src, dst) in enumerate(((w1_in, w1), (w2_in, w2), (wqkv_in, wqkv), (wout_in, wout)))
    ]
    for copy in weights:
        copy.start()

    barrier = pltpu.get_barrier_semaphore()
    for d in range(1, n):
        pl.semaphore_signal(barrier, inc=1, device_id={"gz": lax.rem(me + d, n)}, device_id_type=MESH)

    @pl.when(p > 0)
    def _():
        pl.semaphore_signal(barrier, inc=1, device_id={"xy": p - 1}, device_id_type=MESH)

    @pl.when(p < np_ - 1)
    def _():
        pl.semaphore_signal(barrier, inc=1, device_id={"xy": p + 1}, device_id_type=MESH)

    edge = jnp.zeros((pad, ch), BF16)
    for row in range(count + 4):
        vpad[row, pl.ds(0, pad), :] = edge
        vpad[row, pl.ds(pad + flat, pad), :] = edge
    for row in range(count + 2):
        hpad[row, pl.ds(0, pad), :] = edge
        hpad[row, pl.ds(pad + flat, pad), :] = edge

    @pl.when(p == 0)
    def _():
        vpad[pl.ds(0, 2), pl.ds(pad, flat), :] = jnp.zeros((2, flat, ch), BF16)

    @pl.when(p == np_ - 1)
    def _():
        vpad[pl.ds(count + 2, 2), pl.ds(pad, flat), :] = jnp.zeros((2, flat, ch), BF16)

    extra = jnp.where(p > 0, 1, 0) + jnp.where(p < np_ - 1, 1, 0)
    pl.semaphore_wait(barrier, n - 1 + extra)

    marks = [0] + [min((k + 1) * cells + 2 * pad, flat) for k in range(CHUNKS)]
    ups, downs = [], []
    for k in range(CHUNKS):
        span, held = pl.ds(marks[k], marks[k + 1] - marks[k]), pl.ds(pad + marks[k], marks[k + 1] - marks[k])
        ups.append(pltpu.make_async_remote_copy(
            src_ref=vol.at[pl.ds(0, 2), span], dst_ref=vpad.at[pl.ds(count + 2, 2), held],
            send_sem=halo_send.at[0, k], recv_sem=halo_recv.at[0, k],
            device_id={"xy": p - 1}, device_id_type=MESH,
        ))
        downs.append(pltpu.make_async_remote_copy(
            src_ref=vol.at[pl.ds(count - 2, 2), span], dst_ref=vpad.at[pl.ds(0, 2), held],
            send_sem=halo_send.at[1, k], recv_sem=halo_recv.at[1, k],
            device_id={"xy": p + 1}, device_id_type=MESH,
        ))

    @pl.when(p > 0)
    def _():
        for up in ups:
            up.start()

    @pl.when(p < np_ - 1)
    def _():
        for down in downs:
            down.start()

    weights[0].wait()
    fill_pairs(wide1, w1, ch)
    load.wait()

    done = 0
    for k in range(CHUNKS):
        @pl.when(p > 0)
        def _():
            downs[k].wait_recv()

        @pl.when(p < np_ - 1)
        def _():
            ups[k].wait_recv()

        upto = min((k + 1) * cells + pad, flat)
        size = upto - done
        for pair in range((count + 2) // 2):
            pieces = conv_pair(vpad, 2 * pair, pad + done, size, wide1, ch, sz)
            for i, first in enumerate(pieces):
                row = 2 * pair + i
                half = 0.5 * first
                value = half + half * jnp.tanh(half)
                if row == 0:
                    value = jnp.where(p > 0, value, 0.0)
                if row == count + 1:
                    value = jnp.where(p < np_ - 1, value, 0.0)
                hpad[row, pl.ds(pad + done, size), :] = value.astype(BF16)
        done = upto
        if k == 0:
            weights[1].wait()
            fill_pairs(wide2, w2, ch)
        for pair in range(count // 2):
            pieces = conv_pair(hpad, 2 * pair, pad + k * cells, cells, wide2, ch, sz)
            for i, second in enumerate(pieces):
                row = 2 * pair + i
                base = vpad[row + 2, pl.ds(pad + k * cells, cells), :].astype(F32)
                mixed[row, pl.ds(k * cells, cells), :] = (base + second).astype(BF16)
        for d in range(1, n):
            to = lax.rem(me + d, n)
            start = pl.multiple_of(k * cells + to * unit, unit)
            pltpu.make_async_remote_copy(
                src_ref=mixed.at[:, pl.ds(start, unit)], dst_ref=recv.at[k, me],
                send_sem=fwd_send.at[k], recv_sem=fwd_recv.at[k],
                device_id={"gz": to}, device_id_type=MESH,
            ).start()
        span = pl.ds(k * cells, cells)
        pltpu.make_async_copy(mixed.at[:, span], mixed_out.at[:, span], keep_sem.at[k]).start()
        start = pl.multiple_of(k * cells + me * unit, unit)
        pltpu.make_async_copy(mixed.at[:, pl.ds(start, unit)], recv.at[k, me], own_sem.at[k]).start()

    width = ch // HEADS
    lane = lax.broadcasted_iota(jnp.int32, (n * sz, ch), 1) // width
    masks = [jnp.where(lane == h, 1.0, 0.0).astype(BF16) for h in range(HEADS)]
    ones = jnp.concatenate(masks, axis=0)
    factor = math.log2(math.e) / math.sqrt(width)
    depth = n * sz
    for copy in weights[2:]:
        copy.wait()
    for k in range(CHUNKS):
        others = recv.at[k, pl.ds(0, n - 1)]
        pltpu.make_async_copy(others, others, fwd_recv.at[k]).wait()
        pltpu.make_async_copy(recv.at[k, 0], recv.at[k, 0], own_sem.at[k]).wait()
        for r in range(count):
            block = recv[k, :, r].astype(F32).reshape(n, 2, sz, ch)
            x = jnp.concatenate([block[:, j].reshape(depth, ch) for j in range(2)], axis=0)
            inv = lax.rsqrt(jnp.mean(x * x, axis=-1, keepdims=True) + 1e-6)
            qkv = (jnp.dot(x.astype(BF16), wqkv[...], preferred_element_type=F32) * inv).astype(BF16)
            contexts = []
            for j in range(2):
                q = qkv[j * depth : (j + 1) * depth, :ch]
                key = qkv[j * depth : (j + 1) * depth, ch : 2 * ch]
                v = qkv[j * depth : (j + 1) * depth, 2 * ch :]
                keys = jnp.concatenate([key * m for m in masks], axis=0)
                scores = lax.dot_general(q, keys, (((1,), (1,)), ((), ())), preferred_element_type=F32)
                probs = []
                for h in range(HEADS):
                    s = scores[:, h * depth : (h + 1) * depth]
                    top = jnp.max(s, axis=-1, keepdims=True)
                    probs.append(jnp.exp2((s - top) * factor).astype(BF16))
                values = jnp.concatenate([jnp.concatenate([v * m for m in masks], axis=0), ones], axis=1)
                sums = jnp.dot(jnp.concatenate(probs, axis=1), values, preferred_element_type=F32)
                contexts.append((sums[:, :ch] / sums[:, ch:]).astype(BF16))
            a = jnp.dot(jnp.concatenate(contexts, axis=0), wout[...], preferred_element_type=F32)
            a = jnp.stack([a[:depth].reshape(n, sz, ch), a[depth:].reshape(n, sz, ch)], axis=1)
            att[k, :, r] = a.reshape(n, 2 * sz, ch).astype(BF16)
        spot = pl.multiple_of(k * cells + me * unit, unit)
        for d in range(1, n):
            to = lax.rem(me + d, n)
            pltpu.make_async_remote_copy(
                src_ref=att.at[k, to], dst_ref=ret.at[:, pl.ds(spot, unit)],
                send_sem=bwd_send.at[k], recv_sem=bwd_recv.at[k],
                device_id={"gz": to}, device_id_type=MESH,
            ).start()
        pltpu.make_async_copy(att.at[k, me], ret.at[:, pl.ds(spot, unit)], own_sem.at[k]).start()

    for k in range(CHUNKS):
        others = recv.at[k, pl.ds(0, n - 1)]
        pltpu.make_async_copy(others, others, bwd_recv.at[k]).wait()
        pltpu.make_async_copy(recv.at[k, 0], recv.at[k, 0], own_sem.at[k]).wait()
        span = pl.ds(k * cells, cells)
        pltpu.make_async_copy(mixed.at[:, span], mixed_out.at[:, span], keep_sem.at[k]).wait()
    @pl.when(p > 0)
    def _():
        for up in ups:
            up.wait_send()

    @pl.when(p < np_ - 1)
    def _():
        for down in downs:
            down.wait_send()

    for k in range(CHUNKS):
        others = recv.at[k, pl.ds(0, n - 1)]
        pltpu.make_async_copy(others, others, fwd_send.at[k]).wait()
        pltpu.make_async_copy(others, others, bwd_send.at[k]).wait()


def on_device(volume, conv_first, conv_second, w_qkv, w_out):
    count, wide, sz, ch = volume.shape
    n, np_ = lax.axis_size("gz"), lax.axis_size("xy")
    flat = wide * sz
    unit = flat // CHUNKS // n
    pad = 2 * sz
    mixed, ret = pl.pallas_call(
        functools.partial(kernel, n, np_),
        out_shape=[jax.ShapeDtypeStruct((count, flat, ch), BF16)] * 2,
        in_specs=[pl.BlockSpec(memory_space=pl.ANY)] * 5,
        out_specs=[pl.BlockSpec(memory_space=pl.ANY)] * 2,
        scratch_shapes=[
            pltpu.VMEM(conv_first.shape, BF16),
            pltpu.VMEM(conv_second.shape, BF16),
            pltpu.VMEM(w_qkv.shape, BF16),
            pltpu.VMEM(w_out.shape, BF16),
            pltpu.VMEM((count + 4, flat + 2 * pad, ch), BF16),
            pltpu.VMEM((count + 2, flat + 2 * pad, ch), BF16),
            pltpu.VMEM((count, flat, ch), BF16),
            pltpu.VMEM((4 * ch, 6 * ch), BF16),
            pltpu.VMEM((4 * ch, 6 * ch), BF16),
            pltpu.VMEM((CHUNKS, n, count, unit, ch), BF16),
            pltpu.VMEM((CHUNKS, n, count, unit, ch), BF16),
            pltpu.SemaphoreType.DMA(()),
            pltpu.SemaphoreType.DMA((4,)),
            pltpu.SemaphoreType.DMA((2, CHUNKS)),
            pltpu.SemaphoreType.DMA((2, CHUNKS)),
            pltpu.SemaphoreType.DMA((CHUNKS,)),
            pltpu.SemaphoreType.DMA((CHUNKS,)),
            pltpu.SemaphoreType.DMA((CHUNKS,)),
            pltpu.SemaphoreType.DMA((CHUNKS,)),
            pltpu.SemaphoreType.DMA((CHUNKS,)),
            pltpu.SemaphoreType.DMA((CHUNKS,)),
        ],
        compiler_params=pltpu.CompilerParams(
            collective_id=0, has_side_effects=True, vmem_limit_bytes=60 * 1024 * 1024
        ),
        cost_estimate=pl.CostEstimate(
            flops=2 * count * flat * ch * ch * 24, bytes_accessed=4 * count * flat * ch, transcendentals=0
        ),
    )(volume.reshape(count, flat, ch), conv_first, conv_second, w_qkv, w_out)
    out = (mixed.astype(F32) + ret.astype(F32)).astype(BF16)
    return out.reshape(volume.shape)


def solution(mesh):
    placed = (P("xy", None, "gz", None), P(), P(), P(), P())
    return jax.shard_map(
        on_device, mesh=mesh, in_specs=placed, out_specs=P("xy", None, "gz", None), check_vma=False
    )
```
